32 devices in a mesh: parts: 2 (over y), db: 4 (over z), loop: 4 (over x, core).
Axes of the slice: x: 2, y: 2, z: 4, core: 2. Of those that a mesh axis runs over, the one named last changes fastest.
Arguments:
- queries: bfloat16 [1024, 1024], P(('parts', 'db')), parts along dimension 0, may hold values from -6 to 6
- database: bfloat16 [65536, 1024], P(('parts', 'db', 'loop')), parts along dimension 0, may hold values from -6 to 6
- pair_query: int32 [32, 32], P(('parts', 'db', 'loop')), parts along dimension 0, may hold values from 0 to 3, as said below
- pair_db: int32 [32, 32], P(('parts', 'db', 'loop')), parts along dimension 0, may hold values from 0 to 15, as said below
- pair_count: int32 [32], P(('parts', 'db', 'loop')), parts along dimension 0, may hold values from 16 to 32, as said below
Outputs:
- new_profiles: float32 [1024, 1024], P(('parts', 'db'), 'loop'), parts along dimension 0
The draws below stay inside these ranges and needn't reach their ends.
There are 2 independent parts, one for each index of `parts`. The reference program is written for one: setup_inputs(seed, part) draws one part's arguments, and reference() takes and returns one part's arrays. A program takes and returns all parts, laid end to end along the dimension named above; each array names one. Nothing has to cross between parts.
Inputs may be any that keep to these rules, and one draw needn't show every extreme that they name: `pair_query`: together with pair_db, each row lists 32 distinct pairs of one of the 4 query blocks and one of the 16 database blocks, a subset and order drawn per shard. `pair_db`: see pair_query. Slots at or after pair_count[g] are unused; the count is 32 on some shard and 16 on another in every draw.
All inputs are finite; a program needn't handle non-finite values.
Results may differ from the reference program's by a relative error of at most 0.00082.
Values may be sent and summed in bfloat16 or wider, within the bound.
No kernel may reach another device: no remote copies, remote signals or barrier semaphores. Data moves between devices by JAX's collectives and lax.ppermute only.
A program may use at most 64 MiB of HBM per device.

```python
import math
import jax
import jax.numpy as jnp
from jax import lax

D = 1024
BLK = 128
QBLOCKS = 4
DBBLOCKS = 16
NQ = 512
GROUPS = 16
PAIRS = 32
DBROWS = 32768


def pair_tables(key):
    base = jax.random.fold_in(key, 101)
    subkeys = jax.random.split(base, GROUPS)

    def one_order(subkey):
        return jax.random.permutation(subkey, QBLOCKS * DBBLOCKS)[:PAIRS]
    return jax.vmap(one_order)(subkeys).astype(jnp.int32)


def draw_pair_query(key, part):
    return (pair_tables(key) // DBBLOCKS).astype(jnp.int32)


def draw_pair_db(key, part):
    return (pair_tables(key) % DBBLOCKS).astype(jnp.int32)


def draw_pair_count(key, part):
    counts = jax.random.randint(jax.random.fold_in(key, 202), (GROUPS,), PAIRS // 2, PAIRS + 1, dtype=jnp.int32)
    top_slot = jax.random.randint(jax.random.fold_in(key, 203), (), 0, GROUPS, dtype=jnp.int32)
    offset = jax.random.randint(jax.random.fold_in(key, 204), (), 0, GROUPS - 1, dtype=jnp.int32)
    low_slot = (top_slot + 1 + offset) % GROUPS
    counts = counts.at[top_slot].set(PAIRS)
    counts = counts.at[low_slot].set(PAIRS // 2)
    return counts.astype(jnp.int32)


def level_of(rng, dims, cuts, least, high):
    level, own = 1.0, jax.random.fold_in(rng, 6)
    for position, parts in cuts:
        heights = jnp.exp(jax.random.uniform(jax.random.fold_in(own, position), (parts,), jnp.float32, least / len(cuts), high / len(cuts)))
        level = level * jnp.repeat(heights, dims[position] // parts).reshape([-1 if axis == position else 1 for axis in range(len(dims))])
    return level


def normal_values(key, shape, spread, bound, cuts=(), kind=jnp.bfloat16):
    loudness = level_of(key, shape, cuts, -0.22, 0.18) if cuts else 1.0
    entries = jax.random.normal(key, shape, jnp.float32) * spread * loudness
    return jnp.minimum(jnp.maximum(entries, -bound), bound).astype(kind)


def setup_inputs(seed: int = 0, part: int = 0) -> dict:
    arg_keys = jax.random.split(jax.random.key(seed), 6)
    part_splits = jax.random.split(jax.random.fold_in(arg_keys[5], part), 6)
    return {
        "queries": normal_values(part_splits[0], (NQ, D), 1.0, 6.0, ((0, 4),)),
        "database": normal_values(part_splits[1], (DBROWS, D), 1.0, 6.0, ((0, 16),)),
        "pair_query": draw_pair_query(jax.random.fold_in(jax.random.fold_in(arg_keys[5], part), 71), part),
        "pair_db": draw_pair_db(jax.random.fold_in(jax.random.fold_in(arg_keys[5], part), 71), part),
        "pair_count": draw_pair_count(jax.random.fold_in(jax.random.fold_in(arg_keys[5], part), 71), part),
    }


score_gain = 2.0

def reference(queries, database, pair_query, pair_db, pair_count):
    query_rows, feature_count = queries.shape
    score_scale = score_gain / math.sqrt(feature_count)
    shards = database.reshape(GROUPS, DBBLOCKS * BLK, feature_count)

    def visit_device(state_pair, inputs):
        summed, totals = state_pair
        db_shard, slot_query, slot_db, live_count = inputs
        living = (jnp.arange(PAIRS) < live_count).astype(jnp.float32)
        query_onehot = (slot_query[:, None] == jnp.arange(QBLOCKS)[None, :]).astype(jnp.float32) * living[:, None]
        db_onehot = (slot_db[:, None] == jnp.arange(DBBLOCKS)[None, :]).astype(jnp.float32)
        block_mask = jnp.dot(query_onehot.T, db_onehot, precision=lax.Precision.HIGHEST)
        row_mask = jnp.repeat(jnp.repeat(block_mask, BLK, axis=0), BLK, axis=1)
        scores = jnp.dot(queries, db_shard.T, preferred_element_type=jnp.float32) * score_scale
        weights = jax.nn.sigmoid(scores) * row_mask
        totals = totals + lax.optimization_barrier(jnp.sum(weights, axis=1))
        summed = summed + jnp.dot(weights.astype(jnp.bfloat16), db_shard, preferred_element_type=jnp.float32)
        return ((summed, totals), None)
    start = (jnp.zeros((query_rows, feature_count), jnp.float32), jnp.zeros((query_rows,), jnp.float32))
    (summed, totals), _ = lax.scan(visit_device, start, (shards, pair_query, pair_db, pair_count))
    return queries.astype(jnp.float32) + summed * lax.rsqrt(1.0 + totals)[:, None]
```

```python
import functools
import math

import jax
import jax.numpy as jnp
from jax import lax
from jax.experimental import pallas as pl
from jax.experimental.pallas import tpu as pltpu
from jax.sharding import PartitionSpec as P

BLK = 128
EXTRA = 16
score_gain = 2.0
WIRE = jnp.float16


def block_kernel(scale, meta, own_code, other_code, q_ref, db_ref, other_ref, send_ref, keep_ref,
                 acc, wacc, rows, listing, sems):
    block, side = meta[0], meta[1]
    slots = own_code.shape[1]

    def gather(code_ref, base):
        def step(j, n):
            code = code_ref[0, j]
            listing[n] = base + code % 16
            return n + (code // 16 == block).astype(jnp.int32)
        return step

    n_own = lax.fori_loop(0, slots, gather(own_code, 0), 0)
    n_all = lax.fori_loop(0, slots, gather(other_code, 16), n_own)
    listing[n_all] = listing[jnp.maximum(n_all - 1, 0)]
    steps = (n_all + 1) // 2

    def copy(i, ref):
        start = pl.multiple_of((listing[i] % 16) * BLK, BLK)
        to = pl.multiple_of(i * BLK, BLK)
        return pltpu.make_async_copy(ref.at[pl.ds(start, BLK)], rows.at[pl.ds(to, BLK)], sems.at[i])

    def issue(i, carry):
        @pl.when(listing[i] < 16)
        def _():
            copy(i, db_ref).start()

        @pl.when(listing[i] >= 16)
        def _():
            copy(i, other_ref).start()
        return carry

    lax.fori_loop(0, 2 * steps, issue, 0)
    acc[...] = jnp.zeros_like(acc)
    wacc[...] = jnp.zeros_like(wacc)

    def visit(i, carry):
        copy(2 * i, db_ref).wait()
        copy(2 * i + 1, db_ref).wait()
        tile = rows[pl.ds(pl.multiple_of(i * 2 * BLK, 2 * BLK), 2 * BLK), :]
        s = lax.dot_general(q_ref[...], tile, (((1,), (1,)), ((), ())), preferred_element_type=jnp.float32)
        w = 0.5 * jnp.tanh(s * (0.5 * scale)) + 0.5
        col = lax.broadcasted_iota(jnp.int32, w.shape, 1)
        w = jnp.where(col < (n_all - 2 * i) * BLK, w, 0.0)
        wacc[...] += w[:, :BLK] + w[:, BLK:]
        acc[...] += jnp.dot(w.astype(jnp.bfloat16), tile, preferred_element_type=jnp.float32)
        return carry

    lax.fori_loop(0, steps, visit, 0)
    width = send_ref.shape[1]
    away = pl.multiple_of((1 - side) * width, width)
    here = pl.multiple_of(side * width, width)
    send_ref[pl.ds(0, BLK), :] = acc[:, pl.ds(away, width)]
    keep_ref[pl.ds(0, BLK), :] = acc[:, pl.ds(here, width)]
    totals = jnp.sum(jnp.transpose(wacc[...]), axis=0, keepdims=True)
    totals = jnp.broadcast_to(totals, (EXTRA, BLK))
    totals = jnp.concatenate([totals] * (width // BLK), axis=1)
    send_ref[pl.ds(BLK, EXTRA), :] = totals
    keep_ref[pl.ds(BLK, EXTRA), :] = totals


def block_sums(meta, own_code, other_code, q, db, other, scale):
    width = q.shape[1]
    half = width // 2
    smem = pl.BlockSpec(memory_space=pltpu.SMEM)
    vmem = pl.BlockSpec(memory_space=pltpu.VMEM)
    hbm = pl.BlockSpec(memory_space=pl.ANY)
    most = 2 * own_code.shape[1] // 2 + 2
    return pl.pallas_call(
        functools.partial(block_kernel, scale),
        out_shape=(
            jax.ShapeDtypeStruct((BLK + EXTRA, half), jnp.float32),
            jax.ShapeDtypeStruct((BLK + EXTRA, half), jnp.float32),
        ),
        in_specs=[smem, smem, smem, vmem, hbm, hbm],
        out_specs=(vmem, vmem),
        scratch_shapes=[
            pltpu.VMEM((BLK, width), jnp.float32),
            pltpu.VMEM((BLK, BLK), jnp.float32),
            pltpu.VMEM((most * BLK, width), jnp.bfloat16),
            pltpu.SMEM((most + 2,), jnp.int32),
            pltpu.SemaphoreType.DMA((most,)),
        ],
        compiler_params=pltpu.CompilerParams(vmem_limit_bytes=32 * 1024 * 1024),
        cost_estimate=pl.CostEstimate(flops=2 * 2 * BLK * 2048 * width, bytes_accessed=4 * 1024 * 1024, transcendentals=BLK * 2048),
    )(meta, own_code, other_code, q, db, other)


def final_kernel(keep_ref, got_ref, q_ref, out_ref):
    s = keep_ref[...] + got_ref[...]
    totals = jnp.broadcast_to(s[BLK:BLK + 1, :BLK], (BLK, BLK))
    column = jnp.transpose(totals)
    factor = lax.rsqrt(1.0 + column)
    factor = jnp.concatenate([factor] * (out_ref.shape[1] // BLK), axis=1)
    out_ref[...] = q_ref[...].astype(jnp.float32) + s[:BLK] * factor


def paired(queries, database, pair_query, pair_db, pair_count):
    width = queries.shape[1]
    z = lax.axis_index("db")
    place = lax.axis_index("loop")
    side, core = place // 2, place % 2
    scale = score_gain / math.sqrt(width)
    core_swap = [(i, i ^ 1) for i in range(4)]
    side_swap = [(i, i ^ 2) for i in range(4)]
    near = [(4 * i + j, 4 * (i ^ (j & 1)) + j) for i in range(4) for j in range(4)]
    far = [(4 * i + j, 4 * (i ^ (2 + (j & 1))) + j) for i in range(4) for j in range(4)]
    both = ("db", "loop")

    slot = lax.broadcasted_iota(jnp.int32, pair_query.shape, 1)
    code = jnp.where(slot < pair_count[0], pair_query * 16 + pair_db, -16)
    other = lax.ppermute(database, "loop", core_swap)
    other_code = lax.ppermute(code, "loop", core_swap)
    first = lax.ppermute(queries, both, near)
    second = lax.ppermute(queries, both, far)
    meta1 = jnp.stack([z ^ core, side]).astype(jnp.int32)
    meta2 = jnp.stack([z ^ core ^ 2, side]).astype(jnp.int32)
    send1, keep1 = block_sums(meta1, code, other_code, first, database, other, scale)
    got1 = lax.ppermute(send1.astype(WIRE), "loop", side_swap)
    send2, keep2 = block_sums(meta2, code, other_code, second, database, other, scale)
    got2 = lax.ppermute(send2.astype(WIRE), "loop", side_swap)
    sum1 = (keep1 + got1.astype(jnp.float32)).astype(WIRE)
    in1 = lax.ppermute(sum1, both, near)
    sum2 = (keep2 + got2.astype(jnp.float32)).astype(WIRE)
    in2 = lax.ppermute(sum2, both, far)
    total = in1.astype(jnp.float32) + in2.astype(jnp.float32)
    quarter = width // 4
    given = (lax.dynamic_slice_in_dim(total, (1 - core) * quarter, quarter, 1) * 0.25).astype(WIRE)
    kept = lax.dynamic_slice_in_dim(total, core * quarter, quarter, 1)
    got = lax.ppermute(given, "loop", core_swap).astype(jnp.float32) * 4.0
    own = lax.dynamic_slice_in_dim(queries, place * quarter, quarter, 1)
    return pl.pallas_call(
        final_kernel,
        out_shape=jax.ShapeDtypeStruct((BLK, quarter), jnp.float32),
        in_specs=[pl.BlockSpec(memory_space=pltpu.VMEM)] * 3,
        out_specs=pl.BlockSpec(memory_space=pltpu.VMEM),
    )(kept, got, own)


def per_device(queries, database, pair_query, pair_db, pair_count):
    panels = lax.all_gather(queries, "db", axis=0, tiled=True)
    query_rows, feature_count = panels.shape
    score_scale = score_gain / math.sqrt(feature_count)
    slot_query, slot_db, live_count = pair_query[0], pair_db[0], pair_count[0]

    def visit(slot_no, state_pair):
        summed, totals = state_pair
        query_start = slot_query[slot_no] * BLK
        query_tile = lax.dynamic_slice_in_dim(panels, query_start, BLK, 0)
        db_tile = lax.dynamic_slice_in_dim(database, slot_db[slot_no] * BLK, BLK, 0)
        scores = lax.dot_general(
            query_tile, db_tile, (((1,), (1,)), ((), ())), preferred_element_type=jnp.float32
        ) * score_scale
        weights = jax.nn.sigmoid(scores)
        contrib = jnp.dot(weights.astype(jnp.bfloat16), db_tile, preferred_element_type=jnp.float32)
        old_rows = lax.dynamic_slice_in_dim(summed, query_start, BLK, 0)
        summed = lax.dynamic_update_slice_in_dim(summed, old_rows + contrib, query_start, 0)
        old_totals = lax.dynamic_slice_in_dim(totals, query_start, BLK, 0)
        totals = lax.dynamic_update_slice_in_dim(
            totals, old_totals + jnp.sum(weights, axis=1, keepdims=True), query_start, 0
        )
        return (summed, totals)

    start = (
        jnp.zeros((query_rows, feature_count), jnp.float32),
        jnp.zeros((query_rows, 1), jnp.float32),
    )
    summed_rows, total_rows = lax.fori_loop(0, live_count, visit, start)
    column_width = feature_count // lax.axis_size("loop")
    own_profiles = lax.dynamic_slice_in_dim(
        queries, lax.axis_index("loop") * column_width, column_width, 1
    ).astype(jnp.float32)
    row_sums = lax.psum_scatter(summed_rows, "db", scatter_dimension=0, tiled=True)
    row_weights = lax.psum_scatter(total_rows, "db", scatter_dimension=0, tiled=True)
    partial_out = lax.psum_scatter(row_sums, "loop", scatter_dimension=1, tiled=True)
    weight_out = lax.psum(row_weights, "loop")
    return own_profiles + partial_out * lax.rsqrt(1.0 + weight_out)


def solution(mesh):
    fits = mesh.shape["db"] == 4 and mesh.shape["loop"] == 4
    return jax.shard_map(
        paired if fits else per_device,
        mesh=mesh,
        in_specs=(
            P(("parts", "db"), None),
            P(("parts", "db", "loop"), None),
            P(("parts", "db", "loop"), None),
            P(("parts", "db", "loop"), None),
            P(("parts", "db", "loop")),
        ),
        out_specs=P(("parts", "db"), "loop"),
        check_vma=False,
    )
```

```python
import functools
import math

import jax
import jax.numpy as jnp
from jax import lax
from jax.experimental import pallas as pl
from jax.experimental.pallas import tpu as pltpu
from jax.sharding import PartitionSpec as P

BLK = 128
EXTRA = 8
score_gain = 2.0
WIRE = jnp.float16
SMEM = pl.BlockSpec(memory_space=pltpu.SMEM)
VMEM = pl.BlockSpec(memory_space=pltpu.VMEM)
HBM = pl.BlockSpec(memory_space=pltpu.MemorySpace.HBM)
CHUNKS = 4


def plan_kernel(blocks, meta, own_code, other_code, db_ref, other_ref, rows_ref, plan_ref, sems):
    part = db_ref.shape[0] // CHUNKS
    copies = []
    for shard, ref in enumerate((db_ref, other_ref)):
        for i in range(CHUNKS):
            copies.append(pltpu.make_async_copy(
                ref.at[pl.ds(i * part, part)],
                rows_ref.at[pl.ds((shard * CHUNKS + i) * part, part)],
                sems.at[shard * CHUNKS + i],
            ))
    for copy in copies:
        copy.start()
    slots = own_code.shape[1]
    last = plan_ref.shape[1] - 1
    for which in range(2):
        block = meta[which]
        n = jnp.int32(0)
        for code_ref, base in ((own_code, 0), (other_code, blocks)):
            def step(j, n, code_ref=code_ref, base=base):
                code = code_ref[0, j]
                plan_ref[which, n] = base + (code & 255)
                return n + ((code >> 8) == block).astype(jnp.int32)
            n = lax.fori_loop(0, slots, step, n)
        final = plan_ref[which, jnp.maximum(n - 1, 0)]
        final = jnp.where(n > 0, final, 0)
        for i in range(8):
            plan_ref[which, n + i] = final
        plan_ref[which, last] = n
    for copy in copies:
        copy.wait()


def make_plan(meta, own_code, other_code, db, other):
    slots = own_code.shape[1]
    return pl.pallas_call(
        functools.partial(plan_kernel, db.shape[0] // BLK),
        out_shape=(
            jax.ShapeDtypeStruct((2 * db.shape[0], db.shape[1]), db.dtype),
            jax.ShapeDtypeStruct((2, 2 * slots + 16), jnp.int32),
        ),
        in_specs=[SMEM, SMEM, SMEM, HBM, HBM],
        out_specs=(VMEM, SMEM),
        scratch_shapes=[pltpu.SemaphoreType.DMA((2 * CHUNKS,))],
        compiler_params=pltpu.CompilerParams(vmem_limit_bytes=24 * 1024 * 1024),
        name="plan",
    )(meta, own_code, other_code, db, other)


def block_kernel(scale, which, meta, plan, q_ref, rows_ref, send_ref, keep_ref, acc, wacc):
    side, core = meta[2], meta[3]
    n = plan[which, plan.shape[1] - 1]
    acc[...] = jnp.zeros_like(acc)
    wacc[...] = jnp.zeros_like(wacc)

    def visit(first, group):
        tiles = []
        for g in range(group):
            start = pl.multiple_of(plan[which, first + g] * BLK, BLK)
            tiles.append(rows_ref[pl.ds(start, BLK), :])
        tile = jnp.concatenate(tiles, 0)
        s = lax.dot_general(q_ref[...], tile, (((1,), (1,)), ((), ())), preferred_element_type=jnp.float32)
        w = 0.5 * jnp.tanh(s * (0.5 * scale)) + 0.5
        col = lax.broadcasted_iota(jnp.int32, w.shape, 1)
        w = jnp.where(col < (n - first) * BLK, w, 0.0)
        wsum = wacc[...]
        for g in range(group):
            wsum = wsum + w[:, g * BLK:(g + 1) * BLK]
        wacc[...] = wsum
        acc[...] += jnp.dot(w.astype(jnp.bfloat16), tile, preferred_element_type=jnp.float32)

    wide = (n + 3) // 8

    def step(i, carry):
        visit(8 * i, 8)
        return carry

    lax.fori_loop(0, wide, step, 0)

    @pl.when(8 * wide < n)
    def _():
        visit(8 * wide, 4)

    half = send_ref.shape[1]
    piece = half // 2
    totals = jnp.sum(jnp.transpose(wacc[...]), axis=0, keepdims=True)
    totals = jnp.broadcast_to(totals, (EXTRA, BLK))
    totals = jnp.concatenate([totals] * (piece // BLK), axis=1)
    for ref, x in ((send_ref, 1 - side), (keep_ref, side)):
        for p, c in ((0, core), (1, 1 - core)):
            start = pl.multiple_of(x * half + c * piece, piece)
            ref[pl.ds(0, BLK), pl.ds(p * piece, piece)] = acc[:, pl.ds(start, piece)]
            ref[pl.ds(BLK, EXTRA), pl.ds(p * piece, piece)] = totals


def block_sums(which, meta, plan, q, rows, scale):
    width = q.shape[1]
    half = jax.ShapeDtypeStruct((BLK + EXTRA, width // 2), jnp.float32)
    return pl.pallas_call(
        functools.partial(block_kernel, scale, which),
        out_shape=(half, half),
        in_specs=[SMEM, SMEM, VMEM, VMEM],
        out_specs=(VMEM, VMEM),
        scratch_shapes=[
            pltpu.VMEM((BLK, width), jnp.float32),
            pltpu.VMEM((BLK, BLK), jnp.float32),
        ],
        compiler_params=pltpu.CompilerParams(vmem_limit_bytes=24 * 1024 * 1024),
        cost_estimate=pl.CostEstimate(
            flops=2 * 2 * BLK * 2048 * width, bytes_accessed=1024 * 1024, transcendentals=BLK * 2048),
        name=f"block{which}",
    )(meta, plan, q, rows)


def paired(queries, database, pair_query, pair_db, pair_count):
    width = queries.shape[1]
    z = lax.axis_index("db")
    place = lax.axis_index("loop")
    side, core = place // 2, place % 2
    scale = score_gain / math.sqrt(width)
    both = ("db", "loop")
    grid = [(i, j) for i in range(4) for j in range(4)]
    core_swap = [(j, j ^ 1) for j in range(4)]
    side_swap = [(j, j ^ 2) for j in range(4)]

    def hop(base, turn):
        return [(4 * i + j, 4 * (i ^ (base + (j & 1))) + (j ^ turn)) for i, j in grid]

    slot = lax.broadcasted_iota(jnp.int32, pair_query.shape, 1)
    code = jnp.where(slot < pair_count[0], pair_query * 256 + pair_db, -256)
    other = lax.ppermute(database, "loop", core_swap)
    second = lax.ppermute(queries, both, hop(2, 0))
    first = lax.ppermute(queries, both, hop(0, 0))
    other_code = lax.ppermute(code, "loop", core_swap)
    meta = jnp.stack([z ^ core, z ^ core ^ 2, side, core]).astype(jnp.int32)
    rows, plan = make_plan(meta, code, other_code, database, other)

    send1, keep1 = block_sums(0, meta, plan, first, rows, scale)
    send2, keep2 = block_sums(1, meta, plan, second, rows, scale)
    got1 = lax.ppermute(send1.astype(WIRE), "loop", side_swap)
    got2 = lax.ppermute(send2.astype(WIRE), "loop", side_swap)
    sum2 = (keep2 + got2.astype(jnp.float32)).astype(WIRE)
    sum1 = (keep1 + got1.astype(jnp.float32)).astype(WIRE)
    piece = width // 4
    parts = [
        lax.ppermute(sum2[:, :piece], both, hop(2, 0)),
        lax.ppermute(sum2[:, piece:], both, hop(2, 1)),
        lax.ppermute(sum1[:, :piece], both, hop(0, 0)),
        lax.ppermute(sum1[:, piece:], both, hop(0, 1)),
    ]
    parts = [p.astype(jnp.float32) for p in parts]
    total = (parts[2] + parts[3]) + (parts[0] + parts[1])
    own = lax.dynamic_slice_in_dim(queries, place * piece, piece, 1).astype(jnp.float32)
    return own + total[:BLK] * lax.rsqrt(1.0 + total[BLK, :BLK])[:, None]


def per_device(queries, database, pair_query, pair_db, pair_count):
    if lax.axis_size("db") == 4 and lax.axis_size("loop") == 4 and queries.shape[0] == BLK:
        return paired(queries, database, pair_query, pair_db, pair_count)
    panels = lax.all_gather(queries, "db", axis=0, tiled=True)
    query_rows, feature_count = panels.shape
    score_scale = score_gain / math.sqrt(feature_count)
    slot_query, slot_db, live_count = pair_query[0], pair_db[0], pair_count[0]

    def visit(slot_no, state_pair):
        summed, totals = state_pair
        query_start = slot_query[slot_no] * BLK
        query_tile = lax.dynamic_slice_in_dim(panels, query_start, BLK, 0)
        db_tile = lax.dynamic_slice_in_dim(database, slot_db[slot_no] * BLK, BLK, 0)
        scores = lax.dot_general(
            query_tile, db_tile, (((1,), (1,)), ((), ())), preferred_element_type=jnp.float32
        ) * score_scale
        weights = jax.nn.sigmoid(scores)
        contrib = jnp.dot(weights.astype(jnp.bfloat16), db_tile, preferred_element_type=jnp.float32)
        old_rows = lax.dynamic_slice_in_dim(summed, query_start, BLK, 0)
        summed = lax.dynamic_update_slice_in_dim(summed, old_rows + contrib, query_start, 0)
        old_totals = lax.dynamic_slice_in_dim(totals, query_start, BLK, 0)
        totals = lax.dynamic_update_slice_in_dim(
            totals, old_totals + jnp.sum(weights, axis=1, keepdims=True), query_start, 0
        )
        return (summed, totals)

    start = (
        jnp.zeros((query_rows, feature_count), jnp.float32),
        jnp.zeros((query_rows, 1), jnp.float32),
    )
    summed_rows, total_rows = lax.fori_loop(0, live_count, visit, start)
    column_width = feature_count // lax.axis_size("loop")
    own_profiles = lax.dynamic_slice_in_dim(
        queries, lax.axis_index("loop") * column_width, column_width, 1
    ).astype(jnp.float32)
    row_sums = lax.psum_scatter(summed_rows, "db", scatter_dimension=0, tiled=True)
    row_weights = lax.psum_scatter(total_rows, "db", scatter_dimension=0, tiled=True)
    partial_out = lax.psum_scatter(row_sums, "loop", scatter_dimension=1, tiled=True)
    weight_out = lax.psum(row_weights, "loop")
    return own_profiles + partial_out * lax.rsqrt(1.0 + weight_out)


def solution(mesh):
    return jax.shard_map(
        per_device,
        mesh=mesh,
        in_specs=(
            P(("parts", "db"), None),
            P(("parts", "db", "loop"), None),
            P(("parts", "db", "loop"), None),
            P(("parts", "db", "loop"), None),
            P(("parts", "db", "loop")),
        ),
        out_specs=P(("parts", "db"), "loop"),
        check_vma=False,
    )
```

```python
import functools
import math

import jax
import jax.numpy as jnp
from jax import lax
from jax.experimental import pallas as pl
from jax.experimental.pallas import tpu as pltpu
from jax.sharding import PartitionSpec as P

BLK = 128
EXTRA = 8
score_gain = 2.0
WIRE = jnp.float16
SMEM = pl.BlockSpec(memory_space=pltpu.SMEM)
VMEM = pl.BlockSpec(memory_space=pltpu.VMEM)
HBM = pl.BlockSpec(memory_space=pltpu.MemorySpace.HBM)
GROUP = 8


def plan_kernel(blocks, meta, own_code, other_code, plan_ref):
    last = plan_ref.shape[1] - 1
    counts = [jnp.int32(0), jnp.int32(0)]
    for code_ref, base in ((own_code, 0), (other_code, blocks)):
        for j in range(code_ref.shape[1]):
            code = code_ref[0, j]
            for which in range(2):
                plan_ref[which, counts[which]] = base + (code & 255)
                counts[which] = counts[which] + ((code >> 8) == meta[which]).astype(jnp.int32)
    for which in range(2):
        n = counts[which]
        final = jnp.where(n > 0, plan_ref[which, jnp.maximum(n - 1, 0)], 0)
        for i in range(GROUP):
            plan_ref[which, n + i] = final
        plan_ref[which, last] = n


def make_plan(meta, own_code, other_code, blocks):
    slots = own_code.shape[1]
    return pl.pallas_call(
        functools.partial(plan_kernel, blocks),
        out_shape=jax.ShapeDtypeStruct((2, 2 * slots + 16), jnp.int32),
        in_specs=[SMEM, SMEM, SMEM],
        out_specs=SMEM,
        compiler_params=pltpu.CompilerParams(vmem_limit_bytes=1024 * 1024),
        name="plan",
    )(meta, own_code, other_code)


def block_kernel(scale, which, meta, plan, q_ref, *refs):
    side, core = meta[2], meta[3]
    n = plan[which, plan.shape[1] - 1]
    size = GROUP if which else GROUP // 2
    half_group = GROUP // 2
    if which == 0:
        mine_ref, own_ref, other_ref, send_ref, keep_ref, next_ref, cut_ref, acc, wacc, rows_ref, sems, next_sems, cut_sem = refs
        shard_blocks = own_ref.shape[0] // BLK

        def copy(ref, at, to_ref, i, sem):
            start = pl.multiple_of(at * BLK, BLK)
            to = pl.multiple_of(i * BLK, BLK)
            return pltpu.make_async_copy(ref.at[pl.ds(start, BLK)], to_ref.at[pl.ds(to, BLK)], sem.at[i])

        def fetch(listing, to_ref, sem):
            def issue(i, carry):
                at = plan[listing, i]

                @pl.when(at < shard_blocks)
                def _():
                    copy(own_ref, at, to_ref, i, sem).start()

                @pl.when(at >= shard_blocks)
                def _():
                    copy(other_ref, at - shard_blocks, to_ref, i, sem).start()
                return carry
            count = (plan[listing, plan.shape[1] - 1] + half_group - 1) // half_group * half_group
            lax.fori_loop(0, count, issue, 0)
            return count

        cut = cut_ref.shape[1]
        start = pl.multiple_of((2 * side + core) * cut, cut)
        trim = pltpu.make_async_copy(mine_ref.at[:, pl.ds(start, cut)], cut_ref, cut_sem)
        fetch(0, rows_ref, sems)
        coming = fetch(1, next_ref, next_sems)
        trim.start()
    else:
        rows_ref, send_ref, keep_ref, acc, wacc = refs
    acc[...] = jnp.zeros_like(acc)
    wacc[...] = jnp.zeros_like(wacc)

    def visit(first, group):
        if which == 0:
            for g in range(group):
                copy(own_ref, 0, rows_ref, first + g, sems).wait()
        tile = rows_ref[pl.ds(pl.multiple_of(first * BLK, half_group * BLK), group * BLK), :]
        s = lax.dot_general(q_ref[...], tile, (((1,), (1,)), ((), ())), preferred_element_type=jnp.float32)
        w = 0.5 * jnp.tanh(s * (0.5 * scale)) + 0.5
        col = lax.broadcasted_iota(jnp.int32, w.shape, 1)
        w = jnp.where(col < (n - first) * BLK, w, 0.0)
        wsum = wacc[...]
        for g in range(group):
            wsum = wsum + w[:, g * BLK:(g + 1) * BLK]
        wacc[...] = wsum
        acc[...] += jnp.dot(w.astype(jnp.bfloat16), tile, preferred_element_type=jnp.float32)

    wide = (n + half_group - 1) // size

    def step(i, carry):
        visit(size * i, size)
        return carry

    lax.fori_loop(0, wide, step, 0)

    if size > half_group:
        @pl.when(size * wide < n)
        def _():
            visit(size * wide, half_group)

    half = send_ref.shape[1]
    piece = half // 2
    totals = jnp.sum(jnp.transpose(wacc[...]), axis=0, keepdims=True)
    totals = jnp.broadcast_to(totals, (EXTRA, BLK))
    totals = jnp.concatenate([totals] * (piece // BLK), axis=1)
    for ref, x in ((send_ref, 1 - side), (keep_ref, side)):
        for p, c in ((0, core), (1, 1 - core)):
            start = pl.multiple_of(x * half + c * piece, piece)
            ref[pl.ds(0, BLK), pl.ds(p * piece, piece)] = acc[:, pl.ds(start, piece)]
            ref[pl.ds(BLK, EXTRA), pl.ds(p * piece, piece)] = totals
    if which == 0:
        trim.wait()

        def settle(i, carry):
            copy(own_ref, 0, next_ref, i, next_sems).wait()
            return carry
        lax.fori_loop(0, coming, settle, 0)


def block_sums(which, meta, plan, q, *sources):
    width = q.shape[1]
    scale = score_gain / math.sqrt(width)
    half = jax.ShapeDtypeStruct((BLK + EXTRA, width // 2), jnp.float32)
    outs = [half, half]
    scratch = [pltpu.VMEM((BLK, width), jnp.float32), pltpu.VMEM((BLK, BLK), jnp.float32)]
    if which == 0:
        most = 2 * sources[1].shape[0]
        outs.append(jax.ShapeDtypeStruct((most, width), q.dtype))
        outs.append(jax.ShapeDtypeStruct((BLK, width // 4), q.dtype))
        scratch += [pltpu.VMEM((most, width), q.dtype)] + [pltpu.SemaphoreType.DMA((most // BLK,))] * 2
        scratch.append(pltpu.SemaphoreType.DMA)
    return pl.pallas_call(
        functools.partial(block_kernel, scale, which),
        out_shape=outs,
        in_specs=[SMEM, SMEM, VMEM] + [HBM if which == 0 else VMEM] * len(sources),
        out_specs=[VMEM] * len(outs),
        scratch_shapes=scratch,
        compiler_params=pltpu.CompilerParams(vmem_limit_bytes=(20 if which == 0 else 8) * 1024 * 1024),
        name=f"block{which}",
    )(meta, plan, q, *sources)


def paired(queries, database, pair_query, pair_db, pair_count):
    width = queries.shape[1]
    z = lax.axis_index("db")
    place = lax.axis_index("loop")
    side, core = place // 2, place % 2
    both = ("db", "loop")
    grid = [(i, j) for i in range(4) for j in range(4)]
    core_swap = [(j, j ^ 1) for j in range(4)]
    side_swap = [(j, j ^ 2) for j in range(4)]

    def hop(base, turn):
        return [(4 * i + j, 4 * (i ^ (base + (j & 1))) + (j ^ turn)) for i, j in grid]

    slot = lax.broadcasted_iota(jnp.int32, pair_query.shape, 1)
    code = jnp.where(slot < pair_count[0], pair_query * 256 + pair_db, -256)
    other_code = lax.ppermute(code, "loop", core_swap)
    other = lax.ppermute(database, "loop", core_swap)
    second = lax.ppermute(queries, both, hop(2, 0))
    first = lax.ppermute(queries, both, hop(0, 0))
    meta = jnp.stack([z ^ core, z ^ core ^ 2, side, core]).astype(jnp.int32)
    plan = make_plan(meta, code, other_code, database.shape[0] // BLK)
    away = pltpu.MemorySpace.HBM
    send1, keep1, rows, own = block_sums(
        0, meta, plan, first, pltpu.with_memory_space_constraint(queries, away),
        pltpu.with_memory_space_constraint(database, away),
        pltpu.with_memory_space_constraint(other, away))
    send2, keep2 = block_sums(1, meta, plan, second, rows)
    got1 = lax.ppermute(send1.astype(WIRE), "loop", side_swap)
    got2 = lax.ppermute(send2.astype(WIRE), "loop", side_swap)
    piece = width // 4

    def pass_on(keep, got, turn, base):
        lanes = slice(turn * piece, (turn + 1) * piece)
        summed = (keep[:, lanes] + got[:, lanes].astype(jnp.float32)).astype(WIRE)
        return lax.ppermute(summed, both, hop(base, turn))

    parts = [
        pass_on(keep2, got2, 0, 2),
        pass_on(keep2, got2, 1, 2),
        pass_on(keep1, got1, 0, 0),
        pass_on(keep1, got1, 1, 0),
    ]
    parts = [p.astype(jnp.float32) for p in parts]
    total = (parts[2] + parts[3]) + (parts[0] + parts[1])
    return own.astype(jnp.float32) + total[:BLK] * lax.rsqrt(1.0 + total[BLK, :BLK])[:, None]


def per_device(queries, database, pair_query, pair_db, pair_count):
    if lax.axis_size("db") == 4 and lax.axis_size("loop") == 4 and queries.shape[0] == BLK:
        return paired(queries, database, pair_query, pair_db, pair_count)
    panels = lax.all_gather(queries, "db", axis=0, tiled=True)
    query_rows, feature_count = panels.shape
    score_scale = score_gain / math.sqrt(feature_count)
    slot_query, slot_db, live_count = pair_query[0], pair_db[0], pair_count[0]

    def visit(slot_no, state_pair):
        summed, totals = state_pair
        query_start = slot_query[slot_no] * BLK
        query_tile = lax.dynamic_slice_in_dim(panels, query_start, BLK, 0)
        db_tile = lax.dynamic_slice_in_dim(database, slot_db[slot_no] * BLK, BLK, 0)
        scores = lax.dot_general(
            query_tile, db_tile, (((1,), (1,)), ((), ())), preferred_element_type=jnp.float32
        ) * score_scale
        weights = jax.nn.sigmoid(scores)
        contrib = jnp.dot(weights.astype(jnp.bfloat16), db_tile, preferred_element_type=jnp.float32)
        old_rows = lax.dynamic_slice_in_dim(summed, query_start, BLK, 0)
        summed = lax.dynamic_update_slice_in_dim(summed, old_rows + contrib, query_start, 0)
        old_totals = lax.dynamic_slice_in_dim(totals, query_start, BLK, 0)
        totals = lax.dynamic_update_slice_in_dim(
            totals, old_totals + jnp.sum(weights, axis=1, keepdims=True), query_start, 0
        )
        return (summed, totals)

    start = (
        jnp.zeros((query_rows, feature_count), jnp.float32),
        jnp.zeros((query_rows, 1), jnp.float32),
    )
    summed_rows, total_rows = lax.fori_loop(0, live_count, visit, start)
    column_width = feature_count // lax.axis_size("loop")
    own_profiles = lax.dynamic_slice_in_dim(
        queries, lax.axis_index("loop") * column_width, column_width, 1
    ).astype(jnp.float32)
    row_sums = lax.psum_scatter(summed_rows, "db", scatter_dimension=0, tiled=True)
    row_weights = lax.psum_scatter(total_rows, "db", scatter_dimension=0, tiled=True)
    partial_out = lax.psum_scatter(row_sums, "loop", scatter_dimension=1, tiled=True)
    weight_out = lax.psum(row_weights, "loop")
    return own_profiles + partial_out * lax.rsqrt(1.0 + weight_out)


def solution(mesh):
    return jax.shard_map(
        per_device,
        mesh=mesh,
        in_specs=(
            P(("parts", "db"), None),
            P(("parts", "db", "loop"), None),
            P(("parts", "db", "loop"), None),
            P(("parts", "db", "loop"), None),
            P(("parts", "db", "loop")),
        ),
        out_specs=P(("parts", "db"), "loop"),
        check_vma=False,
    )
```

```python
import functools
import math

import jax
import jax.numpy as jnp
from jax import lax
from jax.experimental import pallas as pl
from jax.experimental.pallas import tpu as pltpu
from jax.sharding import PartitionSpec as P

BLK = 128
EXTRA = 8
score_gain = 2.0
WIRE = jnp.float16
SMEM = pl.BlockSpec(memory_space=pltpu.SMEM)
VMEM = pl.BlockSpec(memory_space=pltpu.VMEM)
HBM = pl.BlockSpec(memory_space=pltpu.MemorySpace.HBM)
GROUP = 8


def fetch_kernel(meta, own_code, other_code, mine_ref, own_ref, other_ref, rows_ref, cut_ref, plan_ref, seen, sems, cut_sem):
    cut = cut_ref.shape[1]
    start = pl.multiple_of((2 * meta[2] + meta[3]) * cut, cut)
    trim = pltpu.make_async_copy(mine_ref.at[:, pl.ds(start, cut)], cut_ref, cut_sem)
    trim.start()
    blocks = own_ref.shape[0] // BLK
    for i in range(2 * blocks):
        seen[i] = 0
    counts = [jnp.int32(0), jnp.int32(0)]

    def copy(ref, at, base):
        start = pl.multiple_of(at * BLK, BLK)
        to = pl.multiple_of((at + base) * BLK, BLK)
        return pltpu.make_async_copy(
            ref.at[pl.ds(start, BLK)], rows_ref.at[pl.ds(to, BLK)], sems.at[at + base])

    for code_ref, ref, base in ((own_code, own_ref, 0), (other_code, other_ref, blocks)):
        for j in range(code_ref.shape[1]):
            code = code_ref[0, j]
            at, block = code & 255, code >> 8
            hits = [(block == meta[which]).astype(jnp.int32) for which in range(2)]
            for which in range(2):
                plan_ref[which, counts[which]] = base + at
                counts[which] = counts[which] + hits[which]

            @pl.when((hits[0] + hits[1] > 0) & (seen[base + at] == 0))
            def _(ref=ref, base=base, at=at):
                seen[base + at] = 1
                copy(ref, at, base).start()

    last = plan_ref.shape[1] - 1
    for which in range(2):
        n = counts[which]
        final = jnp.where(n > 0, plan_ref[which, jnp.maximum(n - 1, 0)], 0)
        for i in range(GROUP):
            plan_ref[which, n + i] = final
        plan_ref[which, last] = n
    for i in range(2 * blocks):
        @pl.when(seen[i] == 1)
        def _(i=i):
            copy(own_ref, 0, i).wait()
    trim.wait()


def fetch(meta, own_code, other_code, mine, own, other):
    width = own.shape[1]
    blocks = own.shape[0] // BLK
    slots = own_code.shape[1]
    return pl.pallas_call(
        fetch_kernel,
        out_shape=(
            jax.ShapeDtypeStruct((2 * own.shape[0], width), own.dtype),
            jax.ShapeDtypeStruct((BLK, width // 4), own.dtype),
            jax.ShapeDtypeStruct((2, 2 * slots + 16), jnp.int32),
        ),
        in_specs=[SMEM, SMEM, SMEM, HBM, HBM, HBM],
        out_specs=(VMEM, VMEM, SMEM),
        scratch_shapes=[
            pltpu.SMEM((2 * blocks,), jnp.int32),
            pltpu.SemaphoreType.DMA((2 * blocks,)),
            pltpu.SemaphoreType.DMA,
        ],
        compiler_params=pltpu.CompilerParams(vmem_limit_bytes=12 * 1024 * 1024),
        name="fetch",
    )(meta, own_code, other_code, mine, own, other)


def block_kernel(scale, which, meta, plan, q_ref, rows_ref, *refs):
    side, core = meta[2], meta[3]
    n = plan[which, plan.shape[1] - 1]
    half_group = GROUP // 2
    if which == 0:
        mine_ref, send_ref, keep_ref, acc, wacc, whole, sem = refs
        bring = pltpu.make_async_copy(mine_ref, whole, sem)

        @pl.when(core == 0)
        def _():
            bring.start()
            bring.wait()

        @pl.when(core == 1)
        def _():
            whole[...] = q_ref[...]
        q_ref = whole
    else:
        send_ref, keep_ref, acc, wacc = refs
    acc[...] = jnp.zeros_like(acc)
    wacc[...] = jnp.zeros_like(wacc)

    def visit(first, group):
        tiles = []
        for g in range(group):
            start = pl.multiple_of(plan[which, first + g] * BLK, BLK)
            tiles.append(rows_ref[pl.ds(start, BLK), :])
        tile = jnp.concatenate(tiles, 0)
        s = lax.dot_general(q_ref[...], tile, (((1,), (1,)), ((), ())), preferred_element_type=jnp.float32)
        w = 0.5 * jnp.tanh(s * (0.5 * scale)) + 0.5
        col = lax.broadcasted_iota(jnp.int32, w.shape, 1)
        w = jnp.where(col < (n - first) * BLK, w, 0.0)
        wsum = wacc[...]
        for g in range(group):
            wsum = wsum + w[:, g * BLK:(g + 1) * BLK]
        wacc[...] = wsum
        acc[...] += jnp.dot(w.astype(jnp.bfloat16), tile, preferred_element_type=jnp.float32)

    wide = (n + half_group - 1) // GROUP

    def step(i, carry):
        visit(GROUP * i, GROUP)
        return carry

    lax.fori_loop(0, wide, step, 0)

    @pl.when(GROUP * wide < n)
    def _():
        visit(GROUP * wide, half_group)

    half = send_ref.shape[1]
    piece = half // 2
    totals = jnp.sum(jnp.transpose(wacc[...]), axis=0, keepdims=True)
    totals = jnp.broadcast_to(totals, (EXTRA, BLK))
    totals = jnp.concatenate([totals] * (piece // BLK), axis=1)
    for ref, x in ((send_ref, 1 - side), (keep_ref, side)):
        for p, c in ((0, core), (1, 1 - core)):
            start = pl.multiple_of(x * half + c * piece, piece)
            ref[pl.ds(0, BLK), pl.ds(p * piece, piece)] = acc[:, pl.ds(start, piece)]
            ref[pl.ds(BLK, EXTRA), pl.ds(p * piece, piece)] = totals


def block_sums(which, meta, plan, q, rows, *mine):
    width = q.shape[1]
    scale = score_gain / math.sqrt(width)
    half = jax.ShapeDtypeStruct((BLK + EXTRA, width // 2), jnp.float32)
    scratch = [pltpu.VMEM((BLK, width), jnp.float32), pltpu.VMEM((BLK, BLK), jnp.float32)]
    if mine:
        scratch += [pltpu.VMEM((BLK, width), q.dtype), pltpu.SemaphoreType.DMA]
    return pl.pallas_call(
        functools.partial(block_kernel, scale, which),
        out_shape=(half, half),
        in_specs=[SMEM, SMEM, VMEM, VMEM] + [HBM] * len(mine),
        out_specs=(VMEM, VMEM),
        scratch_shapes=scratch,
        compiler_params=pltpu.CompilerParams(vmem_limit_bytes=16 * 1024 * 1024),
        name=f"block{which}",
    )(meta, plan, q, rows, *mine)


def paired(queries, database, pair_query, pair_db, pair_count):
    width = queries.shape[1]
    z = lax.axis_index("db")
    place = lax.axis_index("loop")
    side, core = place // 2, place % 2
    both = ("db", "loop")
    grid = [(i, j) for i in range(4) for j in range(4)]
    core_swap = [(j, j ^ 1) for j in range(4)]
    side_swap = [(j, j ^ 2) for j in range(4)]

    def hop(base, turn):
        return [(4 * i + j, 4 * (i ^ (base + (j & 1))) + (j ^ turn)) for i, j in grid]

    slot = lax.broadcasted_iota(jnp.int32, pair_query.shape, 1)
    code = jnp.where(slot < pair_count[0], pair_query * 256 + pair_db, -256)
    other_code = lax.ppermute(code, "loop", core_swap)
    other = lax.ppermute(database, "loop", core_swap)
    second = lax.ppermute(queries, both, hop(2, 0))
    first = lax.ppermute(queries, both, [pair for pair in hop(0, 0) if pair[0] & 1])
    meta = jnp.stack([z ^ core, z ^ core ^ 2, side, core]).astype(jnp.int32)
    away = pltpu.MemorySpace.HBM
    mine = pltpu.with_memory_space_constraint(queries, away)
    rows, own, plan = fetch(
        meta, code, other_code, mine,
        pltpu.with_memory_space_constraint(database, away),
        pltpu.with_memory_space_constraint(other, away))
    send1, keep1 = block_sums(0, meta, plan, first, rows, mine)
    send2, keep2 = block_sums(1, meta, plan, second, rows)
    piece = width // 4
    got1 = lax.ppermute(send1.astype(WIRE), "loop", side_swap)
    got2 = lax.ppermute(send2.astype(WIRE), "loop", side_swap)
    piece = width // 4

    def pieces(keep, got):
        return [
            (keep[:, t * piece:(t + 1) * piece] + got[:, t * piece:(t + 1) * piece].astype(jnp.float32)).astype(WIRE)
            for t in range(2)
        ]

    far, near = pieces(keep2, got2), pieces(keep1, got1)
    parts = [
        lax.ppermute(far[0], both, hop(2, 0)),
        lax.ppermute(far[1], both, hop(2, 1)),
        jnp.where(core == 0, near[0], lax.ppermute(near[0], both, [pair for pair in hop(0, 0) if pair[0] & 1])),
        lax.ppermute(near[1], both, hop(0, 1)),
    ]
    parts = [p.astype(jnp.float32) for p in parts]
    total = (parts[2] + parts[3]) + (parts[0] + parts[1])
    return own.astype(jnp.float32) + total[:BLK] * lax.rsqrt(1.0 + total[BLK, :BLK])[:, None]


def per_device(queries, database, pair_query, pair_db, pair_count):
    if lax.axis_size("db") == 4 and lax.axis_size("loop") == 4 and queries.shape[0] == BLK:
        return paired(queries, database, pair_query, pair_db, pair_count)
    panels = lax.all_gather(queries, "db", axis=0, tiled=True)
    query_rows, feature_count = panels.shape
    score_scale = score_gain / math.sqrt(feature_count)
    slot_query, slot_db, live_count = pair_query[0], pair_db[0], pair_count[0]

    def visit(slot_no, state_pair):
        summed, totals = state_pair
        query_start = slot_query[slot_no] * BLK
        query_tile = lax.dynamic_slice_in_dim(panels, query_start, BLK, 0)
        db_tile = lax.dynamic_slice_in_dim(database, slot_db[slot_no] * BLK, BLK, 0)
        scores = lax.dot_general(
            query_tile, db_tile, (((1,), (1,)), ((), ())), preferred_element_type=jnp.float32
        ) * score_scale
        weights = jax.nn.sigmoid(scores)
        contrib = jnp.dot(weights.astype(jnp.bfloat16), db_tile, preferred_element_type=jnp.float32)
        old_rows = lax.dynamic_slice_in_dim(summed, query_start, BLK, 0)
        summed = lax.dynamic_update_slice_in_dim(summed, old_rows + contrib, query_start, 0)
        old_totals = lax.dynamic_slice_in_dim(totals, query_start, BLK, 0)
        totals = lax.dynamic_update_slice_in_dim(
            totals, old_totals + jnp.sum(weights, axis=1, keepdims=True), query_start, 0
        )
        return (summed, totals)

    start = (
        jnp.zeros((query_rows, feature_count), jnp.float32),
        jnp.zeros((query_rows, 1), jnp.float32),
    )
    summed_rows, total_rows = lax.fori_loop(0, live_count, visit, start)
    column_width = feature_count // lax.axis_size("loop")
    own_profiles = lax.dynamic_slice_in_dim(
        queries, lax.axis_index("loop") * column_width, column_width, 1
    ).astype(jnp.float32)
    row_sums = lax.psum_scatter(summed_rows, "db", scatter_dimension=0, tiled=True)
    row_weights = lax.psum_scatter(total_rows, "db", scatter_dimension=0, tiled=True)
    partial_out = lax.psum_scatter(row_sums, "loop", scatter_dimension=1, tiled=True)
    weight_out = lax.psum(row_weights, "loop")
    return own_profiles + partial_out * lax.rsqrt(1.0 + weight_out)


def solution(mesh):
    return jax.shard_map(
        per_device,
        mesh=mesh,
        in_specs=(
            P(("parts", "db"), None),
            P(("parts", "db", "loop"), None),
            P(("parts", "db", "loop"), None),
            P(("parts", "db", "loop"), None),
            P(("parts", "db", "loop")),
        ),
        out_specs=P(("parts", "db"), "loop"),
        check_vma=False,
    )
```

```python
import functools
import math

import jax
import jax.numpy as jnp
from jax import lax
from jax.experimental import pallas as pl
from jax.experimental.pallas import tpu as pltpu
from jax.sharding import PartitionSpec as P

BLK = 128
EXTRA = 8
score_gain = 2.0
WIRE = jnp.float16
SMEM = pl.BlockSpec(memory_space=pltpu.SMEM)
VMEM = pl.BlockSpec(memory_space=pltpu.VMEM)
HBM = pl.BlockSpec(memory_space=pltpu.MemorySpace.HBM)
GROUP = 8


def fetch_kernel(meta, own_code, other_code, mine_ref, own_ref, other_ref, rows_ref, cut_ref, plan_ref, seen, sems, cut_sem):
    cut = cut_ref.shape[1]
    start = pl.multiple_of((2 * meta[2] + meta[3]) * cut, cut)
    trim = pltpu.make_async_copy(mine_ref.at[:, pl.ds(start, cut)], cut_ref, cut_sem)
    trim.start()
    blocks = own_ref.shape[0] // BLK
    for i in range(2 * blocks):
        seen[i] = 0
    counts = [jnp.int32(0), jnp.int32(0)]

    def copy(ref, at, base):
        start = pl.multiple_of(at * BLK, BLK)
        to = pl.multiple_of((at + base) * BLK, BLK)
        return pltpu.make_async_copy(
            ref.at[pl.ds(start, BLK)], rows_ref.at[pl.ds(to, BLK)], sems.at[at + base])

    for code_ref, ref, base in ((own_code, own_ref, 0), (other_code, other_ref, blocks)):
        for j in range(code_ref.shape[1]):
            code = code_ref[0, j]
            at, block = code & 255, code >> 8
            hits = [(block == meta[which]).astype(jnp.int32) for which in range(2)]
            for which in range(2):
                plan_ref[which, counts[which]] = base + at
                counts[which] = counts[which] + hits[which]

            @pl.when((hits[0] + hits[1] > 0) & (seen[base + at] == 0))
            def _(ref=ref, base=base, at=at):
                seen[base + at] = 1
                copy(ref, at, base).start()

    last = plan_ref.shape[1] - 1
    for which in range(2):
        n = counts[which]
        final = jnp.where(n > 0, plan_ref[which, jnp.maximum(n - 1, 0)], 0)
        for i in range(GROUP):
            plan_ref[which, n + i] = final
        plan_ref[which, last] = n
    for i in range(2 * blocks):
        @pl.when(seen[i] == 1)
        def _(i=i):
            copy(own_ref, 0, i).wait()
    trim.wait()


def fetch(meta, own_code, other_code, mine, own, other):
    width = own.shape[1]
    blocks = own.shape[0] // BLK
    slots = own_code.shape[1]
    return pl.pallas_call(
        fetch_kernel,
        out_shape=(
            jax.ShapeDtypeStruct((2 * own.shape[0], width), own.dtype),
            jax.ShapeDtypeStruct((BLK, width // 4), own.dtype),
            jax.ShapeDtypeStruct((2, 2 * slots + 16), jnp.int32),
        ),
        in_specs=[SMEM, SMEM, SMEM, HBM, HBM, HBM],
        out_specs=(VMEM, VMEM, SMEM),
        scratch_shapes=[
            pltpu.SMEM((2 * blocks,), jnp.int32),
            pltpu.SemaphoreType.DMA((2 * blocks,)),
            pltpu.SemaphoreType.DMA,
        ],
        compiler_params=pltpu.CompilerParams(vmem_limit_bytes=12 * 1024 * 1024),
        name="fetch",
    )(meta, own_code, other_code, mine, own, other)


def block_kernel(scale, which, meta, plan, q_ref, rows_ref, *refs):
    side, core = meta[2], meta[3]
    n = plan[which, plan.shape[1] - 1]
    half_group = GROUP // 2
    if which == 0:
        mine_ref, send_ref, keep_ref, acc, wacc, whole, sem = refs
        bring = pltpu.make_async_copy(mine_ref, whole, sem)

        @pl.when(core == 0)
        def _():
            bring.start()
            bring.wait()

        @pl.when(core == 1)
        def _():
            whole[...] = q_ref[...]
        q_ref = whole
    else:
        send_ref, keep_ref, acc, wacc = refs
    acc[...] = jnp.zeros_like(acc)
    wacc[...] = jnp.zeros_like(wacc)

    def visit(first, group):
        tiles = []
        for g in range(group):
            start = pl.multiple_of(plan[which, first + g] * BLK, BLK)
            tiles.append(rows_ref[pl.ds(start, BLK), :])
        tile = jnp.concatenate(tiles, 0)
        s = lax.dot_general(q_ref[...], tile, (((1,), (1,)), ((), ())), preferred_element_type=jnp.float32)
        w = 0.5 * jnp.tanh(s * (0.5 * scale)) + 0.5
        col = lax.broadcasted_iota(jnp.int32, w.shape, 1)
        w = jnp.where(col < (n - first) * BLK, w, 0.0)
        wsum = wacc[...]
        for g in range(group):
            wsum = wsum + w[:, g * BLK:(g + 1) * BLK]
        wacc[...] = wsum
        acc[...] += jnp.dot(w.astype(jnp.bfloat16), tile, preferred_element_type=jnp.float32)

    wide = (n + half_group - 1) // GROUP

    def step(i, carry):
        visit(GROUP * i, GROUP)
        return carry

    lax.fori_loop(0, wide, step, 0)

    @pl.when(GROUP * wide < n)
    def _():
        visit(GROUP * wide, half_group)

    half = send_ref.shape[1]
    piece = half // 2
    totals = jnp.sum(jnp.transpose(wacc[...]), axis=0, keepdims=True)
    totals = jnp.broadcast_to(totals, (EXTRA, BLK))
    totals = jnp.concatenate([totals] * (piece // BLK), axis=1)
    for ref, x in ((send_ref, 1 - side), (keep_ref, side)):
        for p, c in ((0, core), (1, 1 - core)):
            start = pl.multiple_of(x * half + c * piece, piece)
            ref[pl.ds(0, BLK), pl.ds(p * piece, piece)] = acc[:, pl.ds(start, piece)]
            ref[pl.ds(BLK, EXTRA), pl.ds(p * piece, piece)] = totals


def block_sums(which, meta, plan, q, rows, *mine):
    width = q.shape[1]
    scale = score_gain / math.sqrt(width)
    half = jax.ShapeDtypeStruct((BLK + EXTRA, width // 2), jnp.float32)
    scratch = [pltpu.VMEM((BLK, width), jnp.float32), pltpu.VMEM((BLK, BLK), jnp.float32)]
    if mine:
        scratch += [pltpu.VMEM((BLK, width), q.dtype), pltpu.SemaphoreType.DMA]
    return pl.pallas_call(
        functools.partial(block_kernel, scale, which),
        out_shape=(half, half),
        in_specs=[SMEM, SMEM, VMEM, VMEM] + [HBM] * len(mine),
        out_specs=(VMEM, VMEM),
        scratch_shapes=scratch,
        compiler_params=pltpu.CompilerParams(vmem_limit_bytes=16 * 1024 * 1024),
        name=f"block{which}",
    )(meta, plan, q, rows, *mine)


def paired(queries, database, pair_query, pair_db, pair_count):
    width = queries.shape[1]
    z = lax.axis_index("db")
    place = lax.axis_index("loop")
    side, core = place // 2, place % 2
    both = ("db", "loop")
    grid = [(i, j) for i in range(4) for j in range(4)]
    core_swap = [(j, j ^ 1) for j in range(4)]
    side_swap = [(j, j ^ 2) for j in range(4)]

    def hop(base, turn):
        return [(4 * i + j, 4 * (i ^ (3 - (j & 1) if base else j & 1)) + (j ^ turn)) for i, j in grid]

    slot = lax.broadcasted_iota(jnp.int32, pair_query.shape, 1)
    code = jnp.where(slot < pair_count[0], pair_query * 256 + pair_db, -256)
    other_code = lax.ppermute(code, "loop", core_swap)
    other = lax.ppermute(database, "loop", core_swap)
    second = lax.ppermute(queries, both, hop(2, 0))
    first = lax.ppermute(queries, both, [pair for pair in hop(0, 0) if pair[0] & 1])
    meta = jnp.stack([z ^ core, z ^ (3 - core), side, core]).astype(jnp.int32)
    away = pltpu.MemorySpace.HBM
    mine = pltpu.with_memory_space_constraint(queries, away)
    rows, own, plan = fetch(
        meta, code, other_code, mine,
        pltpu.with_memory_space_constraint(database, away),
        pltpu.with_memory_space_constraint(other, away))
    piece = width // 4
    lanes = [slice(t * piece, (t + 1) * piece) for t in range(2)]
    send2, keep2 = block_sums(1, meta, plan, second, rows)
    first, send2, keep2 = lax.optimization_barrier((first, send2, keep2))
    got2 = lax.ppermute(send2.astype(WIRE), "loop", side_swap)
    send1, keep1 = block_sums(0, meta, plan, first, rows, mine)
    far = [(keep2[:, a] + got2[:, a].astype(jnp.float32)).astype(WIRE) for a in lanes]
    send1, keep1, far = lax.optimization_barrier((send1, keep1, far))
    got1 = lax.ppermute(send1.astype(WIRE), "loop", side_swap)
    near = [(keep1[:, a] + got1[:, a].astype(jnp.float32)).astype(WIRE) for a in lanes]
    only = [pair for pair in hop(0, 0) if pair[0] & 1]
    parts = [lax.ppermute(far[t], both, hop(2, t)) for t in range(2)]
    parts.append(jnp.where(core == 0, near[0], lax.ppermute(near[0], both, only)))
    parts += [lax.ppermute(near[t], both, hop(0, t)) for t in range(1, len(near))]
    parts = [p.astype(jnp.float32) for p in parts]
    total = sum(parts[2:]) + (parts[0] + parts[1])
    return own.astype(jnp.float32) + total[:BLK] * lax.rsqrt(1.0 + total[BLK, :BLK])[:, None]


def per_device(queries, database, pair_query, pair_db, pair_count):
    if lax.axis_size("db") == 4 and lax.axis_size("loop") == 4 and queries.shape[0] == BLK:
        return paired(queries, database, pair_query, pair_db, pair_count)
    panels = lax.all_gather(queries, "db", axis=0, tiled=True)
    query_rows, feature_count = panels.shape
    score_scale = score_gain / math.sqrt(feature_count)
    slot_query, slot_db, live_count = pair_query[0], pair_db[0], pair_count[0]

    def visit(slot_no, state_pair):
        summed, totals = state_pair
        query_start = slot_query[slot_no] * BLK
        query_tile = lax.dynamic_slice_in_dim(panels, query_start, BLK, 0)
        db_tile = lax.dynamic_slice_in_dim(database, slot_db[slot_no] * BLK, BLK, 0)
        scores = lax.dot_general(
            query_tile, db_tile, (((1,), (1,)), ((), ())), preferred_element_type=jnp.float32
        ) * score_scale
        weights = jax.nn.sigmoid(scores)
        contrib = jnp.dot(weights.astype(jnp.bfloat16), db_tile, preferred_element_type=jnp.float32)
        old_rows = lax.dynamic_slice_in_dim(summed, query_start, BLK, 0)
        summed = lax.dynamic_update_slice_in_dim(summed, old_rows + contrib, query_start, 0)
        old_totals = lax.dynamic_slice_in_dim(totals, query_start, BLK, 0)
        totals = lax.dynamic_update_slice_in_dim(
            totals, old_totals + jnp.sum(weights, axis=1, keepdims=True), query_start, 0
        )
        return (summed, totals)

    start = (
        jnp.zeros((query_rows, feature_count), jnp.float32),
        jnp.zeros((query_rows, 1), jnp.float32),
    )
    summed_rows, total_rows = lax.fori_loop(0, live_count, visit, start)
    column_width = feature_count // lax.axis_size("loop")
    own_profiles = lax.dynamic_slice_in_dim(
        queries, lax.axis_index("loop") * column_width, column_width, 1
    ).astype(jnp.float32)
    row_sums = lax.psum_scatter(summed_rows, "db", scatter_dimension=0, tiled=True)
    row_weights = lax.psum_scatter(total_rows, "db", scatter_dimension=0, tiled=True)
    partial_out = lax.psum_scatter(row_sums, "loop", scatter_dimension=1, tiled=True)
    weight_out = lax.psum(row_weights, "loop")
    return own_profiles + partial_out * lax.rsqrt(1.0 + weight_out)


def solution(mesh):
    return jax.shard_map(
        per_device,
        mesh=mesh,
        in_specs=(
            P(("parts", "db"), None),
            P(("parts", "db", "loop"), None),
            P(("parts", "db", "loop"), None),
            P(("parts", "db", "loop"), None),
            P(("parts", "db", "loop")),
        ),
        out_specs=P(("parts", "db"), "loop"),
        check_vma=False,
    )
```
